256 devices in a mesh: row: 8 (over y, core), col: 32 (over z, x).
Axes of the slice: x: 4, y: 4, z: 8, core: 2. Of those that a mesh axis runs over, the one named last changes fastest.
Arguments:
- normed: bfloat16 [1280, 6144], P('col', 'row'), may hold values from -6 to 6
- w_in: bfloat16 [6144, 24576], P('row', 'col'), may hold values from -0.078125 to 0.078125
- w_out: bfloat16 [24576, 6144], P('col', 'row'), may hold values from -0.0390625 to 0.0390625
- out_grad: bfloat16 [1280, 6144], P('col', 'row'), may hold values from -6 to 6
Outputs:
- normed_grad: bfloat16 [1280, 6144], P('col', 'row')
- w_in_grad: float32 [6144, 24576], P('row', 'col')
- w_out_grad: float32 [24576, 6144], P('col', 'row')
The draws below stay inside these ranges and needn't reach their ends.
All inputs are finite; a program needn't handle non-finite values.
Results may differ from the reference program's by a relative error of at most 0.022.
Values may be sent and summed in bfloat16 or wider, within the bound.
No kernel may reach another device: no remote copies, remote signals or barrier semaphores. Data moves between devices by JAX's collectives and lax.ppermute only.
A program may use at most 128 MiB of HBM per device.

```python
import math
import jax
import jax.numpy as jnp

D = 6144
FF = 24576
TOKENS = 1280


def levels(stream_key, extent, split, smallest, high):
    factor_of, own = 1.0, jax.random.fold_in(stream_key, 6)
    for position, blocks in split:
        steps = jnp.exp(jax.random.uniform(jax.random.fold_in(own, position), (blocks,), jnp.float32, smallest / len(split), high / len(split)))
        factor_of = factor_of * jnp.repeat(steps, extent[position] // blocks).reshape([-1 if axis == position else 1 for axis in range(len(extent))])
    return factor_of


def centred(stream_key, extent, deviation, limit, shards=(), kind=jnp.bfloat16):
    gain = levels(stream_key, extent, shards, -0.22, 0.18) if shards else 1.0
    result = jax.random.normal(stream_key, extent, jnp.float32) * deviation * gain
    return jnp.minimum(jnp.maximum(result, -limit), limit).astype(kind)


def setup_inputs(seed: int = 0) -> dict:
    key_of = jax.random.split(jax.random.key(seed), 5)
    return {
        "normed": centred(key_of[0], (TOKENS, D), 1.0, 6.0, ((0, 32), (1, 8))),
        "w_in": centred(key_of[1], (D, FF), D ** -0.5, 0.078125, ((0, 8), (1, 32))),
        "w_out": centred(key_of[2], (FF, D), FF ** -0.5, 0.0390625, ((0, 32), (1, 8))),
        "out_grad": centred(key_of[3], (TOKENS, D), 1.0, 6.0, ((0, 32), (1, 8))),
    }


def gelu_parts(preact):
    normal_cdf = 0.5 * (1.0 + jax.scipy.special.erf(preact * (1.0 / math.sqrt(2.0))))
    density = jnp.exp(-0.5 * preact * preact) * (1.0 / math.sqrt(2.0 * math.pi))
    return (preact * normal_cdf, normal_cdf + preact * density)

def reference(normed, w_in, w_out, out_grad):
    preact = jnp.dot(normed, w_in, preferred_element_type=jnp.float32)
    act_grad = jnp.dot(out_grad, w_out.T, preferred_element_type=jnp.float32)
    activation, gelu_slope = gelu_parts(preact)
    hidden = activation.astype(jnp.bfloat16)
    hidden_grad = (act_grad * gelu_slope).astype(jnp.bfloat16)
    grad_scale = float(TOKENS) ** (-0.5)
    w_in_grad = jnp.dot(normed.T, hidden_grad, preferred_element_type=jnp.float32) * grad_scale
    w_out_grad = jnp.dot(hidden.T, out_grad, preferred_element_type=jnp.float32) * grad_scale
    normed_grad = jnp.dot(hidden_grad, w_in.T, preferred_element_type=jnp.float32).astype(jnp.bfloat16)
    return (normed_grad, w_in_grad, w_out_grad)
```

```python
import math

import jax
import jax.numpy as jnp
from jax import lax
from jax.sharding import PartitionSpec as P

NZ, NX, NY, NC = 8, 4, 4, 2
BF16, F32 = jnp.bfloat16, jnp.float32


def z_shift(step):
    return [(NX * z + x, NX * ((z + step) % NZ) + x) for z in range(NZ) for x in range(NX)]


def x_shift(step):
    return [(NX * z + x, NX * z + (x + step) % NX) for z in range(NZ) for x in range(NX)]


def y_shift(step):
    return [(NC * y + c, NC * ((y + step) % NY) + c) for y in range(NY) for c in range(NC)]


CORE_SWAP = [(r, r ^ 1) for r in range(NY * NC)]


def send_z(value, step):
    return lax.ppermute(value, "col", z_shift(step))


def send_x(value, step):
    return lax.ppermute(value, "col", x_shift(step))


def send_y(value, step):
    return lax.ppermute(value, "row", y_shift(step))


def swap_core(value):
    return lax.ppermute(value, "row", CORE_SWAP)


def ring_gather(block, send, n):
    got = [None] * n
    got[0] = block
    up = down = block
    for k in range(1, n // 2):
        up, down = send(up, 1), send(down, -1)
        got[n - k], got[k] = up, down
    half = block.shape[0] // 2
    got[n // 2] = jnp.concatenate([send(up[:half], 1), send(down[half:], -1)], axis=0)
    return got


def ring_reduce(parts, send, n):
    far = parts(n // 2)
    half = far.shape[0] // 2
    up, down = send(far[:half].astype(BF16), 1), send(far[half:].astype(BF16), -1)
    for k in range(n // 2 - 1, 0, -1):
        ahead, behind = parts(k), parts(n - k)
        if k == n // 2 - 1:
            ahead = jnp.concatenate([ahead[:half] + up.astype(F32), ahead[half:]], axis=0)
            behind = jnp.concatenate([behind[:half], behind[half:] + down.astype(F32)], axis=0)
        else:
            ahead, behind = ahead + up.astype(F32), behind + down.astype(F32)
        up, down = send(ahead.astype(BF16), 1), send(behind.astype(BF16), -1)
    return parts(0) + up.astype(F32) + down.astype(F32)


def direct_reduce(parts, send, n):
    return sum(
        (send(parts(d).astype(BF16), d).astype(F32) for d in range(1, n)), parts(0).astype(F32)
    )


def gelu_parts(preact):
    normal_cdf = 0.5 * (1.0 + jax.scipy.special.erf(preact * (1.0 / math.sqrt(2.0))))
    density = jnp.exp(-0.5 * preact * preact) * (1.0 / math.sqrt(2.0 * math.pi))
    return (preact * normal_cdf, normal_cdf + preact * density)


def hidden_pair(preact, act_grad):
    activation, gelu_slope = gelu_parts(preact)
    return (activation.astype(BF16), (act_grad * gelu_slope).astype(BF16))


def per_device(normed, w_in, w_out, out_grad):
    rows, width = normed.shape
    tokens = rows * NZ * NX
    row = lax.axis_index("row")
    y, c = row // NC, row % NC
    half, quarter = tokens // NC, tokens // NC // NY

    near = jnp.concatenate([normed] + [send_x(normed, -e) for e in range(1, NX)], axis=0)
    rows_all = jnp.concatenate(ring_gather(near, send_z, NZ), axis=0)
    line = jnp.concatenate(ring_gather(out_grad, send_z, NZ), axis=0)
    grad_all = (
        jnp.stack([part.reshape(NZ, rows, width) for part in ring_gather(line, send_x, NX)], axis=1)
    ).reshape(tokens, width)

    def summed_over_row(product):
        away = product(lax.dynamic_slice_in_dim, (1 - c) * half).astype(BF16)
        kept = product(lax.dynamic_slice_in_dim, c * half)
        pair = kept + swap_core(away).astype(F32)
        return ring_reduce(
            lambda d: lax.dynamic_slice_in_dim(pair, ((y + d) % NY) * quarter, quarter, 0), send_y, NY
        )

    preact = summed_over_row(
        lambda cut, at: jnp.dot(cut(rows_all, at, half, 0), w_in, preferred_element_type=F32)
    )
    act_grad = summed_over_row(
        lambda cut, at: lax.dot_general(
            cut(grad_all, at, half, 0), w_out, (((1,), (1,)), ((), ())), preferred_element_type=F32
        )
    )
    hidden_share, grad_share = hidden_pair(preact, act_grad)

    def spread_over_row(share):
        got = ring_gather(share, send_y, NY)
        twice = jnp.concatenate(got + got, axis=0)
        mine = lax.dynamic_slice_in_dim(twice, ((NY - y) % NY) * quarter, half, 0)
        other = swap_core(mine)
        return jnp.where(
            c == 0,
            jnp.concatenate([mine, other], axis=0),
            jnp.concatenate([other, mine], axis=0),
        )

    hidden_grad = spread_over_row(grad_share)
    hidden = spread_over_row(hidden_share)
    grad_scale = float(tokens) ** (-0.5)
    partial = lax.dot_general(
        hidden_grad, w_in, (((1,), (1,)), ((), ())), preferred_element_type=F32
    )
    w_in_grad = (
        lax.dot_general(
            rows_all, hidden_grad, (((0,), (0,)), ((), ())), preferred_element_type=F32
        )
        * grad_scale
    )
    w_out_grad = (
        lax.dot_general(hidden, grad_all, (((0,), (0,)), ((), ())), preferred_element_type=F32)
        * grad_scale
    )

    grid = partial.reshape(NZ, NX, rows, width)
    left, right = grid[..., : width // 2], grid[..., width // 2 :]
    left_grid = left
    left = ring_reduce(lambda d: left_of(left_grid, d, rows), send_z, NZ).reshape(NX, rows, width // 2)
    left_line = left
    left = direct_reduce(lambda e: left_line[e], send_x, NX)
    right_grid = right
    right = ring_reduce(lambda e: right_grid[:, e].reshape(NZ * rows, width // 2), send_x, NX)
    right = right.reshape(NZ, rows, width // 2)
    right_line = right
    right = ring_reduce(lambda d: right_line[d], send_z, NZ)
    normed_grad = jnp.concatenate([left, right], axis=1).astype(BF16)
    return (normed_grad, w_in_grad, w_out_grad)


def left_of(grid, d, rows):
    return grid[d].reshape(NX * rows, -1)


def solution(mesh):
    in_specs = (P("col", "row"), P("row", "col"), P("col", "row"), P("col", "row"))
    out_specs = (P("col", "row"), P("row", "col"), P("col", "row"))
    return jax.shard_map(
        per_device, mesh=mesh, in_specs=in_specs, out_specs=out_specs, check_vma=False
    )
```

```python
import functools
import math

import jax
import jax.numpy as jnp
from jax import lax
from jax.experimental import pallas as pl
from jax.experimental.pallas import tpu as pltpu
from jax.sharding import PartitionSpec as P

NZ, NX, NY, NC = 8, 4, 4, 2
BF16, F32 = jnp.bfloat16, jnp.float32
VMEM_BYTES = 40 * 1024 * 1024

GROUPS = ((1, 7, 2, 6), (0, 4, 3, 5))


def z_shift(step):
    return [(NX * z + x, NX * ((z + step) % NZ) + x) for z in range(NZ) for x in range(NX)]


def x_shift(step):
    return [(NX * z + x, NX * z + (x + step) % NX) for z in range(NZ) for x in range(NX)]


def y_shift(step):
    return [(NC * y + c, NC * ((y + step) % NY) + c) for y in range(NY) for c in range(NC)]


CORE_SWAP = [(r, r ^ 1) for r in range(NY * NC)]


def send_z(value, step):
    return lax.ppermute(value, "col", z_shift(step))


def send_x(value, step):
    return lax.ppermute(value, "col", x_shift(step))


def send_y(value, step):
    return lax.ppermute(value, "row", y_shift(step))


def swap_core(value):
    return lax.ppermute(value, "row", CORE_SWAP)


def on_core(kernel, outs, *operands):
    return pl.pallas_call(
        kernel,
        out_shape=[jax.ShapeDtypeStruct(shape, dtype) for shape, dtype in outs],
        in_specs=[pl.BlockSpec(memory_space=pltpu.SMEM)]
        + [pl.BlockSpec(memory_space=pltpu.VMEM)] * (len(operands) - 1),
        out_specs=[pl.BlockSpec(memory_space=pltpu.VMEM)] * len(outs),
        compiler_params=pltpu.CompilerParams(vmem_limit_bytes=VMEM_BYTES),
    )(*operands)


def contract(a, b, dims):
    return lax.dot_general(a, b, ((dims[:1], dims[1:]), ((), ())), preferred_element_type=F32)


def gelu_parts(preact):
    normal_cdf = 0.5 * (1.0 + lax.erf(preact * (1.0 / math.sqrt(2.0))))
    density = jnp.exp(-0.5 * preact * preact) * (1.0 / math.sqrt(2.0 * math.pi))
    return (preact * normal_cdf, normal_cdf + preact * density)


def project(counts, place, *refs):
    pieces, (w_in, w_out, kept, away) = refs[: sum(counts)], refs[sum(counts) :]
    core = place[1]
    width = w_in.shape[0]
    half = w_in.shape[1] // 2
    mine = core == 0
    in_low, in_high = w_in[:, :half], w_in[:, half:]
    out_low, out_high = w_out[:half, :], w_out[half:, :]
    in_kept, in_away = jnp.where(mine, in_low, in_high), jnp.where(mine, in_high, in_low)
    out_kept, out_away = jnp.where(mine, out_low, out_high), jnp.where(mine, out_high, out_low)
    at = 0
    for chunk, count in enumerate(counts):
        row = 0
        for piece in pieces[at : at + count]:
            rows = piece.shape[0]
            normed, grad = piece[:, :width], piece[:, width:]
            here = pl.ds(row, rows)
            away[chunk, here, :half] = contract(normed, in_away, (1, 0)).astype(BF16)
            away[chunk, here, half:] = contract(grad, out_away, (1, 1)).astype(BF16)
            kept[chunk, here, :half] = contract(normed, in_kept, (1, 0))
            kept[chunk, here, half:] = contract(grad, out_kept, (1, 1))
            row += rows
        at += count


def pair_sum(place, kept, other, far_up, far_down, ahead, behind, own):
    y = place[0]
    half = far_up.shape[0]

    def pair(step):
        q = lax.rem(y + step, NY)
        return kept[q] + other[q].astype(F32)

    far = pair(2).astype(BF16)
    far_up[...] = far[:half]
    far_down[...] = far[half:]
    ahead[...] = pair(1)
    behind[...] = pair(3)
    own[...] = pair(0)


def pass_on(place, ahead, behind, got_up, got_down, next_up, next_down):
    half = got_up.shape[0]
    next_up[:half] = (ahead[:half] + got_up[...].astype(F32)).astype(BF16)
    next_up[half:] = ahead[half:].astype(BF16)
    next_down[:half] = behind[:half].astype(BF16)
    next_down[half:] = (behind[half:] + got_down[...].astype(F32)).astype(BF16)


def activate(place, own, got_up, got_down, hidden_grad, hidden):
    half = hidden.shape[1]
    total = own[...] + got_up[...].astype(F32) + got_down[...].astype(F32)
    activation, slope = gelu_parts(total[:, :half])
    hidden[...] = activation.astype(BF16)
    hidden_grad[...] = (total[:, half:] * slope).astype(BF16)


def assemble(place, own, up, down, far_up, far_down, out):
    y = place[0]
    half = far_up.shape[0]
    out[y] = own[...]
    out[lax.rem(y + 3, NY)] = up[...]
    out[lax.rem(y + 1, NY)] = down[...]
    far = lax.rem(y + 2, NY)
    out[far, :half] = far_up[...]
    out[far, half:] = far_down[...]


def backward(place, *refs):
    groups = len(GROUPS)
    mine, theirs = refs[:groups], refs[groups : 2 * groups]
    w_in, out = refs[2 * groups :]
    core = place[1]
    half = w_in.shape[1] // 2
    low, high = w_in[:, :half], w_in[:, half:]
    first, second = jnp.where(core == 0, low, high), jnp.where(core == 0, high, low)
    for g in range(groups):
        for k in range(NY):
            out[g * NY + k] = contract(mine[g][k], first, (1, 1)) + contract(
                theirs[g][k], second, (1, 1)
            )


def weight_grads(scale, counts, place, *refs):
    groups = len(GROUPS)
    total = sum(counts)
    pieces, refs = refs[:total], refs[total:]
    hidden_mine, hidden_theirs = refs[:groups], refs[groups : 2 * groups]
    grad_mine, grad_theirs = refs[2 * groups : 3 * groups], refs[3 * groups : 4 * groups]
    w_in_grad, w_out_grad, rows_all, grad_all = refs[4 * groups :]
    width = w_in_grad.shape[0]
    row = 0
    for piece in pieces:
        rows = piece.shape[0]
        rows_all[pl.ds(row, rows)] = piece[:, :width]
        grad_all[pl.ds(row, rows)] = piece[:, width:]
        row += rows
    core = place[1]
    half = w_in_grad.shape[1] // 2
    own, other = pl.ds(core * half, half), pl.ds((1 - core) * half, half)

    def joined(parts):
        return jnp.concatenate([part[k] for part in parts for k in range(NY)], axis=0)

    for side, grads, hiddens in ((own, grad_mine, hidden_mine), (other, grad_theirs, hidden_theirs)):
        w_in_grad[:, side] = contract(rows_all[...], joined(grads), (0, 0)) * scale
        w_out_grad[side, :] = contract(joined(hiddens), grad_all[...], (0, 0)) * scale


def per_device(normed, w_in, w_out, out_grad):
    rows, width = normed.shape
    chunk = rows * NX
    tokens = chunk * NZ
    hidden_units = w_in.shape[1]
    half_units = hidden_units // NC
    half = chunk // 2
    row = lax.axis_index("row")
    place = jnp.stack([row // NC, row % NC]).astype(jnp.int32)

    both = jnp.concatenate([normed, out_grad], axis=1)
    near = jnp.concatenate([both] + [send_x(both, -e) for e in range(1, NX)], axis=0)
    chunks = [None] * NZ
    chunks[0] = [near]
    up = down = near
    for k in range(1, NZ // 2):
        up, down = send_z(up, 1), send_z(down, -1)
        chunks[NZ - k], chunks[k] = [up], [down]
    chunks[NZ // 2] = [send_z(up[:half], 1), send_z(down[half:], -1)]

    def row_sum(group):
        pieces = [piece for d in group for piece in chunks[d]]
        counts = tuple(len(chunks[d]) for d in group)
        kept, away = on_core(
            functools.partial(project, counts),
            [((NY, chunk, 2 * half_units), F32), ((NY, chunk, 2 * half_units), BF16)],
            place, *pieces, w_in, w_out,
        )
        far_up, far_down, ahead, behind, own = on_core(
            pair_sum,
            [((half, 2 * half_units), BF16)] * 2 + [((chunk, 2 * half_units), F32)] * 3,
            place, kept, swap_core(away),
        )
        next_up, next_down = on_core(
            pass_on,
            [((chunk, 2 * half_units), BF16)] * 2,
            place, ahead, behind, send_y(far_up, 1), send_y(far_down, -1),
        )
        return on_core(
            activate,
            [((chunk, half_units), BF16)] * 2,
            place, own, send_y(next_up, 1), send_y(next_down, -1),
        )

    def row_spread(share):
        up, down = send_y(share, 1), send_y(share, -1)
        far_up, far_down = send_y(up[:half], 1), send_y(down[half:], -1)
        (mine,) = on_core(
            assemble, [((NY,) + share.shape, BF16)], place, share, up, down, far_up, far_down
        )
        return mine, swap_core(mine)

    shares = [row_sum(group) for group in GROUPS]
    grads = [row_spread(share[0]) for share in shares]
    (partial,) = on_core(
        backward,
        [((NZ, chunk, width), F32)],
        place, *[g[0] for g in grads], *[g[1] for g in grads], w_in,
    )
    hiddens = [row_spread(share[1]) for share in shares]
    order = [d for group in GROUPS for d in group]
    pieces = [piece for d in order for piece in chunks[d]]
    w_in_grad, w_out_grad = weight_call(
        tokens, place, pieces, hiddens, grads, w_in.shape, w_out.shape
    )

    part = lambda d: partial[order.index(d)]
    far = part(NZ // 2)
    up, down = send_z(far[:half].astype(BF16), 1), send_z(far[half:].astype(BF16), -1)
    for k in range(NZ // 2 - 1, 0, -1):
        ahead, behind = part(k), part(NZ - k)
        if up.shape[0] == half:
            ahead = jnp.concatenate([ahead[:half] + up.astype(F32), ahead[half:]], axis=0)
            behind = jnp.concatenate([behind[:half], behind[half:] + down.astype(F32)], axis=0)
        else:
            ahead, behind = ahead + up.astype(F32), behind + down.astype(F32)
        up, down = send_z(ahead.astype(BF16), 1), send_z(behind.astype(BF16), -1)
    line = (part(0) + up.astype(F32) + down.astype(F32)).reshape(NX, rows, width)
    total = line[0]
    for e in range(1, NX):
        total = total + send_x(line[e].astype(BF16), e).astype(F32)
    return (total.astype(BF16), w_in_grad, w_out_grad)


def weight_call(tokens, place, pieces, hiddens, grads, in_shape, out_shape):
    operands = (
        list(pieces)
        + [h[0] for h in hiddens]
        + [h[1] for h in hiddens]
        + [g[0] for g in grads]
        + [g[1] for g in grads]
    )
    width = in_shape[0]
    return pl.pallas_call(
        functools.partial(weight_grads, float(tokens) ** (-0.5), (1,) * len(pieces)),
        out_shape=[jax.ShapeDtypeStruct(in_shape, F32), jax.ShapeDtypeStruct(out_shape, F32)],
        in_specs=[pl.BlockSpec(memory_space=pltpu.SMEM)]
        + [pl.BlockSpec(memory_space=pltpu.VMEM)] * len(operands),
        out_specs=[pl.BlockSpec(memory_space=pltpu.VMEM)] * 2,
        scratch_shapes=[pltpu.VMEM((tokens, width), BF16)] * 2,
        compiler_params=pltpu.CompilerParams(vmem_limit_bytes=VMEM_BYTES),
    )(place, *operands)


def solution(mesh):
    in_specs = (P("col", "row"), P("row", "col"), P("col", "row"), P("col", "row"))
    out_specs = (P("col", "row"), P("row", "col"), P("col", "row"))
    return jax.shard_map(
        per_device, mesh=mesh, in_specs=in_specs, out_specs=out_specs, check_vma=False
    )
```

```python
import functools
import math

import jax
import jax.numpy as jnp
from jax import lax
from jax.experimental import pallas as pl
from jax.experimental.pallas import tpu as pltpu
from jax.sharding import PartitionSpec as P

NZ, NX, NY, NC = 8, 4, 4, 2
BF16, F32 = jnp.bfloat16, jnp.float32
VMEM_BYTES = 40 * 1024 * 1024

PLACES = ((1, 7), (2, 6), (0, 4), (3, 5))
ORDER = [d for pair in PLACES for d in pair]
EARLY = 2


def z_shift(step):
    return [(NX * z + x, NX * ((z + step) % NZ) + x) for z in range(NZ) for x in range(NX)]


def x_shift(step):
    return [(NX * z + x, NX * z + (x + step) % NX) for z in range(NZ) for x in range(NX)]


def y_shift(step):
    return [(NC * y + c, NC * ((y + step) % NY) + c) for y in range(NY) for c in range(NC)]


CORE_SWAP = [(r, r ^ 1) for r in range(NY * NC)]


def send_z(value, step):
    return lax.ppermute(value, "col", z_shift(step))


def send_x(value, step):
    return lax.ppermute(value, "col", x_shift(step))


def send_y(value, step):
    return lax.ppermute(value, "row", y_shift(step))


def swap_core(value):
    return lax.ppermute(value, "row", CORE_SWAP)


def cost(flops, *arrays):
    return pl.CostEstimate(
        flops=flops,
        transcendentals=0,
        bytes_accessed=sum(math.prod(a.shape) * a.dtype.itemsize for a in arrays),
    )


def on_core(kernel, outs, *operands, flops=0):
    shapes = [jax.ShapeDtypeStruct(shape, dtype) for shape, dtype in outs]
    return pl.pallas_call(
        kernel,
        cost_estimate=cost(flops, *operands, *shapes),
        name=getattr(kernel, "func", kernel).__name__,
        out_shape=shapes,
        in_specs=[pl.BlockSpec(memory_space=pltpu.SMEM)]
        + [pl.BlockSpec(memory_space=pltpu.VMEM)] * (len(operands) - 1),
        out_specs=[pl.BlockSpec(memory_space=pltpu.VMEM)] * len(outs),
        compiler_params=pltpu.CompilerParams(vmem_limit_bytes=VMEM_BYTES),
    )(*operands)


def contract(a, b, dims):
    return lax.dot_general(a, b, ((dims[:1], dims[1:]), ((), ())), preferred_element_type=F32)


def gelu_parts(preact):
    normal_cdf = 0.5 * (1.0 + lax.erf(preact * (1.0 / math.sqrt(2.0))))
    density = jnp.exp(-0.5 * preact * preact) * (1.0 / math.sqrt(2.0 * math.pi))
    return (preact * normal_cdf, normal_cdf + preact * density)


def project(counts, place, *refs):
    pieces, (w_in, w_out, kept, away) = refs[: sum(counts)], refs[sum(counts) :]
    core = place[1]
    width = w_in.shape[0]
    half = w_in.shape[1] // 2
    mine = core == 0
    in_low, in_high = w_in[:, :half], w_in[:, half:]
    out_low, out_high = w_out[:half, :], w_out[half:, :]
    in_kept, in_away = jnp.where(mine, in_low, in_high), jnp.where(mine, in_high, in_low)
    out_kept, out_away = jnp.where(mine, out_low, out_high), jnp.where(mine, out_high, out_low)
    at = 0
    for chunk, count in enumerate(counts):
        row = 0
        for piece in pieces[at : at + count]:
            rows = piece.shape[0]
            normed, grad = piece[:, :width], piece[:, width:]
            here = pl.ds(row, rows)
            away[chunk, here, :half] = contract(normed, in_away, (1, 0)).astype(BF16)
            away[chunk, here, half:] = contract(grad, out_away, (1, 1)).astype(BF16)
            kept[chunk, here, :half] = contract(normed, in_kept, (1, 0))
            kept[chunk, here, half:] = contract(grad, out_kept, (1, 1))
            row += rows
        at += count


def pair_sum(place, kept_0, kept_1, other_0, other_1, far_up, far_down, ahead, behind, own):
    y = place[0]

    def pair(step, which):
        q = lax.rem(y + step, NY)
        at = lax.rem(q, EARLY) * 2 + which
        return jnp.where(
            q < EARLY,
            kept_0[at] + other_0[at].astype(F32),
            kept_1[at] + other_1[at].astype(F32),
        )

    far_up[...] = pair(2, 0).astype(BF16)
    far_down[...] = pair(2, 1).astype(BF16)
    for which in range(2):
        ahead[which] = pair(1, which)
        behind[which] = pair(3, which)
        own[which] = pair(0, which)


def pass_on(place, ahead, behind, got_up, got_down, next_up, next_down):
    next_up[0] = (ahead[0] + got_up[...].astype(F32)).astype(BF16)
    next_up[1] = ahead[1].astype(BF16)
    next_down[0] = behind[0].astype(BF16)
    next_down[1] = (behind[1] + got_down[...].astype(F32)).astype(BF16)


def activate(place, own, got_up, got_down, hidden_grad, hidden):
    half = hidden.shape[2]
    for which in range(2):
        total = own[which] + got_up[which].astype(F32) + got_down[which].astype(F32)
        activation, slope = gelu_parts(total[:, :half])
        hidden[which] = activation.astype(BF16)
        hidden_grad[which] = (total[:, half:] * slope).astype(BF16)


def assemble(place, own, up, down, far_up, far_down, out):
    y = place[0]
    far = lax.rem(y + 2, NY) * 2
    for which in range(2):
        out[y * 2 + which] = own[which]
        out[lax.rem(y + 3, NY) * 2 + which] = up[which]
        out[lax.rem(y + 1, NY) * 2 + which] = down[which]
    out[far] = far_up[0]
    out[far + 1] = far_down[0]


def backward_first(place, mine, w_in, out):
    half = w_in.shape[1] // 2
    weight = jnp.where(place[1] == 0, w_in[:, :half], w_in[:, half:])
    for k in range(NZ):
        out[k] = contract(mine[k], weight, (1, 1))


def backward_second(place, first, theirs, w_in, far, out):
    half = w_in.shape[1] // 2
    weight = jnp.where(place[1] == 0, w_in[:, half:], w_in[:, :half])
    for k in range(NZ):
        total = first[k] + contract(theirs[k], weight, (1, 1))
        if ORDER[k] == NZ // 2:
            far[0] = total[: far.shape[1]].astype(BF16)
            far[1] = total[far.shape[1] :].astype(BF16)
        else:
            out[k] = total


def weight_grad(scale, total, hidden_first, place, *refs):
    pieces, (mine, theirs, out, tokens_all) = refs[:total], refs[total:]
    width = tokens_all.shape[1]
    row = 0
    for piece in pieces:
        rows = piece.shape[0]
        tokens_all[pl.ds(row, rows)] = piece[:, width:] if hidden_first else piece[:, :width]
        row += rows
    core = place[1]
    half = mine.shape[2]
    for parts, at in ((mine, core * half), (theirs, (1 - core) * half)):
        joined = jnp.concatenate([parts[k] for k in range(NZ)], axis=0)
        side = pl.ds(pl.multiple_of(at, half), half)
        if hidden_first:
            out[side, :] = contract(joined, tokens_all[...], (0, 0)) * scale
        else:
            out[:, side] = contract(tokens_all[...], joined, (0, 0)) * scale


def after(value, *earlier):
    return lax.optimization_barrier((value, earlier))[0]


def per_device(normed, w_in, w_out, out_grad):
    rows, width = normed.shape
    chunk = rows * NX
    tokens = chunk * NZ
    units = w_in.shape[1]
    half_units = units // NC
    half = chunk // 2
    row = lax.axis_index("row")
    place = jnp.stack([row // NC, row % NC]).astype(jnp.int32)

    def project_group(group):
        pieces = [piece for d in group for piece in chunks[d]]
        counts = tuple(len(chunks[d]) for d in group)
        return on_core(
            functools.partial(project, counts),
            [((len(group), chunk, units), F32), ((len(group), chunk, units), BF16)],
            place, *pieces, w_in, w_out,
        )

    both = jnp.concatenate([normed, out_grad], axis=1)
    near = jnp.concatenate([both] + [send_x(both, -e) for e in range(1, NX)], axis=0)
    chunks = [None] * NZ
    chunks[0] = [near]
    up = down = near
    for k in range(1, NZ // 2):
        up, down = send_z(up, 1), send_z(down, -1)
        chunks[NZ - k], chunks[k] = [up], [down]
    kept_0, away_0 = project_group(ORDER[: 2 * EARLY])
    up, down, away_0 = lax.optimization_barrier((up, down, away_0))
    chunks[NZ // 2 + 1], chunks[NZ // 2 - 1] = [up], [down]
    chunks[NZ // 2] = [send_z(up[:half], 1), send_z(down[half:], -1)]
    other_0 = swap_core(away_0)
    kept_1, away_1 = project_group(ORDER[2 * EARLY :])
    other_1 = swap_core(away_1)
    far_up, far_down, ahead, behind, own = on_core(
        pair_sum,
        [((chunk, units), BF16)] * 2 + [((2, chunk, units), F32)] * 3,
        place, kept_0, kept_1, other_0, other_1,
    )
    next_up, next_down = on_core(
        pass_on,
        [((2, chunk, units), BF16)] * 2,
        place, ahead, behind, send_y(far_up, 1), send_y(far_down, -1),
    )
    grad_share, hidden_share = on_core(
        activate,
        [((2, chunk, half_units), BF16)] * 2,
        place, own, send_y(next_up, 1), send_y(next_down, -1),
    )

    def gathered(share, near, far):
        return on_core(assemble, [((NZ,) + share.shape[1:], BF16)], place, share, *near, *far)[0]

    near_grad = send_y(grad_share, 1), send_y(grad_share, -1)
    far_grad = send_y(near_grad[0][:1], 1), send_y(near_grad[1][1:], -1)
    grad_mine = gathered(grad_share, near_grad, far_grad)
    grad_theirs = swap_core(grad_mine)
    (first,) = on_core(
        backward_first, [((NZ, chunk, width), F32)], place, grad_mine, w_in
    )
    far, partial = on_core(
        backward_second,
        [((2, half, width), BF16), ((NZ, chunk, width), F32)],
        place, first, grad_theirs, w_in,
    )

    pieces = [piece for d in ORDER for piece in chunks[d]]
    scale = float(tokens) ** (-0.5)

    def weight_call(hidden_first, shape, mine, theirs):
        operands = pieces + [mine, theirs]
        result = jax.ShapeDtypeStruct(shape, F32)
        return pl.pallas_call(
            functools.partial(weight_grad, scale, len(pieces), hidden_first),
            cost_estimate=cost(2 * tokens * shape[0] * shape[1], result, *operands),
            name="weight_grad",
            out_shape=result,
            in_specs=[pl.BlockSpec(memory_space=pltpu.SMEM)]
            + [pl.BlockSpec(memory_space=pltpu.VMEM)] * len(operands),
            out_specs=pl.BlockSpec(memory_space=pltpu.VMEM),
            scratch_shapes=[pltpu.VMEM((tokens, width), BF16)],
            compiler_params=pltpu.CompilerParams(vmem_limit_bytes=VMEM_BYTES),
        )(after(place, partial), *operands)

    part = lambda d: partial[ORDER.index(d)]
    up, down = send_z(far[0], 1), send_z(far[1], -1)
    w_in_grad = weight_call(False, w_in.shape, grad_mine, grad_theirs)
    up, down, w_in_grad = lax.optimization_barrier((up, down, w_in_grad))
    hidden_share = after(hidden_share, up)
    near_hidden = send_y(hidden_share, 1), send_y(hidden_share, -1)
    for k in range(NZ // 2 - 1, 0, -1):
        ahead, behind = part(k), part(NZ - k)
        if up.shape[0] == half:
            ahead = jnp.concatenate([ahead[:half] + up.astype(F32), ahead[half:]], axis=0)
            behind = jnp.concatenate([behind[:half], behind[half:] + down.astype(F32)], axis=0)
        else:
            ahead, behind = ahead + up.astype(F32), behind + down.astype(F32)
        up, down = send_z(ahead.astype(BF16), 1), send_z(behind.astype(BF16), -1)
        if k == 3:
            up, down, near_hidden = lax.optimization_barrier((up, down, near_hidden))
            far_hidden = send_y(near_hidden[0][:1], 1), send_y(near_hidden[1][1:], -1)
        if k == 2:
            hidden_mine = gathered(hidden_share, near_hidden, far_hidden)
            up, down, hidden_mine = lax.optimization_barrier((up, down, hidden_mine))
            hidden_theirs = swap_core(hidden_mine)
    w_out_grad = weight_call(True, w_out.shape, hidden_mine, hidden_theirs)
    up, down, hidden_theirs = lax.optimization_barrier((up, down, hidden_theirs))
    line = (part(0) + up.astype(F32) + down.astype(F32)).reshape(NX, rows, width)
    total = line[0]
    for e in range(1, NX):
        total = total + send_x(line[e].astype(BF16), e).astype(F32)
    return (total.astype(BF16), w_in_grad, w_out_grad)


def solution(mesh):
    in_specs = (P("col", "row"), P("row", "col"), P("col", "row"), P("col", "row"))
    out_specs = (P("col", "row"), P("row", "col"), P("col", "row"))
    return jax.shard_map(
        per_device, mesh=mesh, in_specs=in_specs, out_specs=out_specs, check_vma=False
    )
```

```python
import functools
import math

import jax
import jax.numpy as jnp
from jax import lax
from jax.experimental import pallas as pl
from jax.experimental.pallas import tpu as pltpu
from jax.sharding import PartitionSpec as P

NZ, NX, NY, NC = 8, 4, 4, 2
BF16, F32 = jnp.bfloat16, jnp.float32
VMEM_BYTES = 40 * 1024 * 1024

PLACES = ((1, 7), (2, 6), (0, 4), (3, 5))
ORDER = [d for pair in PLACES for d in pair]
EARLY = 2


def z_shift(step):
    return [(NX * z + x, NX * ((z + step) % NZ) + x) for z in range(NZ) for x in range(NX)]


def x_shift(step):
    return [(NX * z + x, NX * z + (x + step) % NX) for z in range(NZ) for x in range(NX)]


def y_shift(step):
    return [(NC * y + c, NC * ((y + step) % NY) + c) for y in range(NY) for c in range(NC)]


CORE_SWAP = [(r, r ^ 1) for r in range(NY * NC)]


def send_z(value, step):
    return lax.ppermute(value, "col", z_shift(step))


def send_x(value, step):
    return lax.ppermute(value, "col", x_shift(step))


def send_y(value, step):
    return lax.ppermute(value, "row", y_shift(step))


def swap_core(value):
    return lax.ppermute(value, "row", CORE_SWAP)


def cost(flops, *arrays):
    return pl.CostEstimate(
        flops=flops,
        transcendentals=0,
        bytes_accessed=sum(math.prod(a.shape) * a.dtype.itemsize for a in arrays),
    )


def on_core(kernel, outs, *operands, flops=0):
    shapes = [jax.ShapeDtypeStruct(shape, dtype) for shape, dtype in outs]
    return pl.pallas_call(
        kernel,
        cost_estimate=cost(flops, *operands, *shapes),
        name=getattr(kernel, "func", kernel).__name__,
        out_shape=shapes,
        in_specs=[pl.BlockSpec(memory_space=pltpu.SMEM)]
        + [pl.BlockSpec(memory_space=pltpu.VMEM)] * (len(operands) - 1),
        out_specs=[pl.BlockSpec(memory_space=pltpu.VMEM)] * len(outs),
        compiler_params=pltpu.CompilerParams(vmem_limit_bytes=VMEM_BYTES),
    )(*operands)


def contract(a, b, dims):
    return lax.dot_general(a, b, ((dims[:1], dims[1:]), ((), ())), preferred_element_type=F32)


def gelu_parts(preact):
    normal_cdf = 0.5 * (1.0 + lax.erf(preact * (1.0 / math.sqrt(2.0))))
    density = jnp.exp(-0.5 * preact * preact) * (1.0 / math.sqrt(2.0 * math.pi))
    return (preact * normal_cdf, normal_cdf + preact * density)


def project(counts, place, *refs):
    pieces, (w_in, w_out, kept, away) = refs[: sum(counts)], refs[sum(counts) :]
    core = place[1]
    width = w_in.shape[0]
    half = w_in.shape[1] // 2
    mine = core == 0
    in_low, in_high = w_in[:, :half], w_in[:, half:]
    out_low, out_high = w_out[:half, :], w_out[half:, :]
    in_kept, in_away = jnp.where(mine, in_low, in_high), jnp.where(mine, in_high, in_low)
    out_kept, out_away = jnp.where(mine, out_low, out_high), jnp.where(mine, out_high, out_low)
    chunks, rows = kept.shape[:2]
    normed = jnp.concatenate([piece[:, :width] for piece in pieces], axis=0)
    grad = jnp.concatenate([piece[:, width:] for piece in pieces], axis=0)

    def store(out, side, value):
        for k in range(chunks):
            out[k, :, side] = value[k * rows : (k + 1) * rows].astype(out.dtype)

    left, right = pl.ds(0, half), pl.ds(half, half)
    store(away, left, contract(normed, in_away, (1, 0)))
    store(away, right, contract(grad, out_away, (1, 1)))
    store(kept, left, contract(normed, in_kept, (1, 0)))
    store(kept, right, contract(grad, out_kept, (1, 1)))


def pair_sum(
    place, kept_0, kept_1, other_0, other_1,
    far_up, far_down, free_up, free_down, held_up, held_down, own,
):
    y = place[0]

    def pair(step, which):
        q = lax.rem(y + step, NY)
        at = lax.rem(q, EARLY) * 2 + which
        return jnp.where(
            q < EARLY,
            kept_0[at] + other_0[at].astype(F32),
            kept_1[at] + other_1[at].astype(F32),
        )

    far_up[...] = pair(2, 0).astype(BF16)
    far_down[...] = pair(2, 1).astype(BF16)
    free_up[...] = pair(1, 1).astype(BF16)
    free_down[...] = pair(3, 0).astype(BF16)
    held_up[...] = pair(1, 0)
    held_down[...] = pair(3, 1)
    for which in range(2):
        own[which] = pair(0, which)


def pass_on(place, held_up, held_down, got_up, got_down, next_up, next_down):
    next_up[...] = (held_up[...] + got_up[...].astype(F32)).astype(BF16)
    next_down[...] = (held_down[...] + got_down[...].astype(F32)).astype(BF16)


def activate(place, own, up_0, up_1, down_0, down_1, hidden_grad, hidden):
    half = hidden.shape[2]
    for which, up, down in ((0, up_0, down_0), (1, up_1, down_1)):
        total = own[which] + up[...].astype(F32) + down[...].astype(F32)
        activation, slope = gelu_parts(total[:, :half])
        hidden[which] = activation.astype(BF16)
        hidden_grad[which] = (total[:, half:] * slope).astype(BF16)


def assemble(place, own, up, down, far_up, far_down, out):
    y = place[0]
    far = lax.rem(y + 2, NY) * 2
    for which in range(2):
        out[y * 2 + which] = own[which]
        out[lax.rem(y + 3, NY) * 2 + which] = up[which]
        out[lax.rem(y + 1, NY) * 2 + which] = down[which]
    out[far] = far_up[0]
    out[far + 1] = far_down[0]


def backward_first(place, mine, w_in, out):
    half = w_in.shape[1] // 2
    weight = jnp.where(place[1] == 0, w_in[:, :half], w_in[:, half:])
    for k in range(NZ):
        out[k] = contract(mine[k], weight, (1, 1))


def backward_second(place, first, theirs, w_in, far, out):
    half = w_in.shape[1] // 2
    weight = jnp.where(place[1] == 0, w_in[:, half:], w_in[:, :half])
    for k in range(NZ):
        total = first[k] + contract(theirs[k], weight, (1, 1))
        if ORDER[k] == NZ // 2:
            far[0] = total[: far.shape[1]].astype(BF16)
            far[1] = total[far.shape[1] :].astype(BF16)
        else:
            out[k] = total


def weight_grad(scale, total, hidden_first, place, *refs):
    pieces, (mine, theirs, out, tokens_all) = refs[:total], refs[total:]
    width = tokens_all.shape[1]
    row = 0
    for piece in pieces:
        rows = piece.shape[0]
        tokens_all[pl.ds(row, rows)] = piece[:, width:] if hidden_first else piece[:, :width]
        row += rows
    core = place[1]
    half = mine.shape[2]
    for parts, at in ((mine, core * half), (theirs, (1 - core) * half)):
        joined = jnp.concatenate([parts[k] for k in range(NZ)], axis=0)
        side = pl.ds(pl.multiple_of(at, half), half)
        if hidden_first:
            out[side, :] = contract(joined, tokens_all[...], (0, 0)) * scale
        else:
            out[:, side] = contract(tokens_all[...], joined, (0, 0)) * scale


def after(value, *earlier):
    return lax.optimization_barrier((value, earlier))[0]


def per_device(normed, w_in, w_out, out_grad):
    rows, width = normed.shape
    chunk = rows * NX
    tokens = chunk * NZ
    units = w_in.shape[1]
    half_units = units // NC
    half = chunk // 2
    row = lax.axis_index("row")
    place = jnp.stack([row // NC, row % NC]).astype(jnp.int32)

    def project_group(group):
        pieces = [piece for d in group for piece in chunks[d]]
        counts = tuple(len(chunks[d]) for d in group)
        return on_core(
            functools.partial(project, counts),
            [((len(group), chunk, units), F32), ((len(group), chunk, units), BF16)],
            place, *pieces, w_in, w_out,
        )

    both = jnp.where(
        lax.broadcasted_iota(jnp.int32, (rows, 2 * width), 1) < width,
        jnp.pad(normed, ((0, 0), (0, width))),
        jnp.pad(out_grad, ((0, 0), (width, 0))),
    )
    line = [both] + [send_x(both, -e) for e in range(1, NX)]
    chunks = [[None, None] for _ in range(NZ)]
    for part in range(2):
        chunks[0][part] = jnp.concatenate(line[2 * part : 2 * part + 2], axis=0)
    for k in range(1, NZ // 2):
        for part in range(2):
            chunks[NZ - k][part] = send_z(chunks[(NZ + 1 - k) % NZ][part], 1)
            chunks[k][part] = send_z(chunks[k - 1][part], -1)
    kept_0, away_0 = project_group(ORDER[: 2 * EARLY])
    up, down = chunks[NZ // 2 + 1], chunks[NZ // 2 - 1]
    last = [send_z(up[0], 1), send_z(down[1], -1)]
    last, away_0 = lax.optimization_barrier((last, away_0))
    chunks[NZ // 2] = last
    other_0 = swap_core(away_0)
    kept_1, away_1 = project_group(ORDER[2 * EARLY :])
    other_1 = swap_core(away_1)
    far_up, far_down, free_up, free_down, held_up, held_down, own = on_core(
        pair_sum,
        [((chunk, units), BF16)] * 4 + [((chunk, units), F32)] * 2 + [((2, chunk, units), F32)],
        place, kept_0, kept_1, other_0, other_1,
    )
    got_up, got_down = send_y(far_up, 1), send_y(far_down, -1)
    free_up, free_down = send_y(free_up, 1), send_y(free_down, -1)
    next_up, next_down = on_core(
        pass_on, [((chunk, units), BF16)] * 2, place, held_up, held_down, got_up, got_down
    )
    grad_share, hidden_share = on_core(
        activate,
        [((2, chunk, half_units), BF16)] * 2,
        place, own, send_y(next_up, 1), free_up, free_down, send_y(next_down, -1),
    )

    def gathered(share, near, far):
        return on_core(assemble, [((NZ,) + share.shape[1:], BF16)], place, share, *near, *far)[0]

    near_grad = send_y(grad_share, 1), send_y(grad_share, -1)
    far_grad = send_y(near_grad[0][:1], 1), send_y(near_grad[1][1:], -1)
    grad_mine = gathered(grad_share, near_grad, far_grad)
    grad_theirs = swap_core(grad_mine)
    (first,) = on_core(
        backward_first, [((NZ, chunk, width), F32)], place, grad_mine, w_in
    )
    far, partial = on_core(
        backward_second,
        [((2, half, width), BF16), ((NZ, chunk, width), F32)],
        place, first, grad_theirs, w_in,
    )

    pieces = [piece for d in ORDER for piece in chunks[d]]
    scale = float(tokens) ** (-0.5)

    def weight_call(hidden_first, shape, mine, theirs):
        operands = pieces + [mine, theirs]
        result = jax.ShapeDtypeStruct(shape, F32)
        return pl.pallas_call(
            functools.partial(weight_grad, scale, len(pieces), hidden_first),
            cost_estimate=cost(2 * tokens * shape[0] * shape[1], result, *operands),
            name="weight_grad",
            out_shape=result,
            in_specs=[pl.BlockSpec(memory_space=pltpu.SMEM)]
            + [pl.BlockSpec(memory_space=pltpu.VMEM)] * len(operands),
            out_specs=pl.BlockSpec(memory_space=pltpu.VMEM),
            scratch_shapes=[pltpu.VMEM((tokens, width), BF16)],
            compiler_params=pltpu.CompilerParams(vmem_limit_bytes=VMEM_BYTES),
        )(after(place, partial), *operands)

    part = lambda d: partial[ORDER.index(d)]
    up, down = send_z(far[0], 1), send_z(far[1], -1)
    w_in_grad = weight_call(False, w_in.shape, grad_mine, grad_theirs)
    up, down, w_in_grad = lax.optimization_barrier((up, down, w_in_grad))
    hidden_share = after(hidden_share, up)
    near_hidden = send_y(hidden_share, 1), send_y(hidden_share, -1)
    for k in range(NZ // 2 - 1, 0, -1):
        ahead, behind = part(k), part(NZ - k)
        if up.shape[0] == half:
            ahead = jnp.concatenate([ahead[:half] + up.astype(F32), ahead[half:]], axis=0)
            behind = jnp.concatenate([behind[:half], behind[half:] + down.astype(F32)], axis=0)
        else:
            ahead, behind = ahead + up.astype(F32), behind + down.astype(F32)
        up, down = send_z(ahead.astype(BF16), 1), send_z(behind.astype(BF16), -1)
        if k == 3:
            up, down, near_hidden = lax.optimization_barrier((up, down, near_hidden))
            far_hidden = send_y(near_hidden[0][:1], 1), send_y(near_hidden[1][1:], -1)
        if k == 2:
            hidden_mine = gathered(hidden_share, near_hidden, far_hidden)
            up, down, hidden_mine = lax.optimization_barrier((up, down, hidden_mine))
            hidden_theirs = swap_core(hidden_mine)
    w_out_grad = weight_call(True, w_out.shape, hidden_mine, hidden_theirs)
    up, down, hidden_theirs = lax.optimization_barrier((up, down, hidden_theirs))
    line = (part(0) + up.astype(F32) + down.astype(F32)).reshape(NX, rows, width)
    total = line[0]
    for e in range(1, NX):
        total = total + send_x(line[e].astype(BF16), e).astype(F32)
    return (total.astype(BF16), w_in_grad, w_out_grad)


def solution(mesh):
    in_specs = (P("col", "row"), P("row", "col"), P("col", "row"), P("col", "row"))
    out_specs = (P("col", "row"), P("row", "col"), P("col", "row"))
    return jax.shard_map(
        per_device, mesh=mesh, in_specs=in_specs, out_specs=out_specs, check_vma=False
    )
```

```python
import functools
import math

import jax
import jax.numpy as jnp
from jax import lax
from jax.experimental import pallas as pl
from jax.experimental.pallas import tpu as pltpu
from jax.sharding import PartitionSpec as P

NZ, NX, NY, NC = 8, 4, 4, 2
BF16, F32 = jnp.bfloat16, jnp.float32
VMEM_BYTES = 40 * 1024 * 1024

PLACES = ((1, 7), (2, 6), (0, 4), (3, 5))
ORDER = [d for pair in PLACES for d in pair]
ROUNDS = ((1, 7, 2, 6), (0, 3, 5), (4,))


def z_shift(step):
    return [(NX * z + x, NX * ((z + step) % NZ) + x) for z in range(NZ) for x in range(NX)]


def x_shift(step):
    return [(NX * z + x, NX * z + (x + step) % NX) for z in range(NZ) for x in range(NX)]


def y_shift(step):
    return [(NC * y + c, NC * ((y + step) % NY) + c) for y in range(NY) for c in range(NC)]


CORE_SWAP = [(r, r ^ 1) for r in range(NY * NC)]


def send_z(value, step):
    return lax.ppermute(value, "col", z_shift(step))


def send_x(value, step):
    return lax.ppermute(value, "col", x_shift(step))


def send_y(value, step):
    return lax.ppermute(value, "row", y_shift(step))


def swap_core(value):
    return lax.ppermute(value, "row", CORE_SWAP)


def cost(flops, *arrays):
    return pl.CostEstimate(
        flops=flops,
        transcendentals=0,
        bytes_accessed=sum(math.prod(a.shape) * a.dtype.itemsize for a in arrays),
    )


def on_core(kernel, outs, *operands, flops=0):
    shapes = [jax.ShapeDtypeStruct(shape, dtype) for shape, dtype in outs]
    return pl.pallas_call(
        kernel,
        cost_estimate=cost(flops, *operands, *shapes),
        name=getattr(kernel, "func", kernel).__name__,
        out_shape=shapes,
        in_specs=[pl.BlockSpec(memory_space=pltpu.SMEM)]
        + [pl.BlockSpec(memory_space=pltpu.VMEM)] * (len(operands) - 1),
        out_specs=[pl.BlockSpec(memory_space=pltpu.VMEM)] * len(outs),
        compiler_params=pltpu.CompilerParams(vmem_limit_bytes=VMEM_BYTES),
    )(*operands)


def contract(a, b, dims):
    return lax.dot_general(a, b, ((dims[:1], dims[1:]), ((), ())), preferred_element_type=F32)


def gelu_parts(preact):
    normal_cdf = 0.5 * (1.0 + lax.erf(preact * (1.0 / math.sqrt(2.0))))
    density = jnp.exp(-0.5 * preact * preact) * (1.0 / math.sqrt(2.0 * math.pi))
    return (preact * normal_cdf, normal_cdf + preact * density)


def split_weights(place, w_in, w_out, in_kept, in_away, out_kept, out_away):
    half = in_kept.shape[1]
    mine = place[1] == 0
    in_low, in_high = w_in[:, :half], w_in[:, half:]
    out_low, out_high = w_out[:half, :], w_out[half:, :]
    in_kept[...], in_away[...] = jnp.where(mine, in_low, in_high), jnp.where(mine, in_high, in_low)
    out_kept[...] = jnp.where(mine, out_low, out_high)
    out_away[...] = jnp.where(mine, out_high, out_low)


def project(counts, place, *refs):
    pieces, (in_kept, in_away, out_kept, out_away, kept, away) = (
        refs[: sum(counts)], refs[sum(counts) :]
    )
    width, half = in_kept.shape
    chunks, rows = kept.shape[:2]
    normed = jnp.concatenate([piece[:, :width] for piece in pieces], axis=0)
    grad = jnp.concatenate([piece[:, width:] for piece in pieces], axis=0)

    def store(out, side, value):
        for k in range(chunks):
            out[k, :, side] = value[k * rows : (k + 1) * rows].astype(out.dtype)

    left, right = pl.ds(0, half), pl.ds(half, half)
    store(away, left, contract(normed, in_away[...], (1, 0)))
    store(away, right, contract(grad, out_away[...], (1, 1)))
    store(kept, left, contract(normed, in_kept[...], (1, 0)))
    store(kept, right, contract(grad, out_kept[...], (1, 1)))


def pair_sum(
    place, kept_0, kept_1, kept_2, other_0, other_1, other_2,
    far_up, far_down, free_up, free_down, held_up, held_down, own,
):
    y = place[0]

    def chunk_sum(kept, other, at):
        return kept[at] + other[at].astype(F32)

    def pair(step, which):
        q = lax.rem(y + step, NY)
        early = chunk_sum(kept_0, other_0, lax.rem(q, 2) * 2 + which)
        if which == 0:
            late = chunk_sum(kept_1, other_1, lax.rem(q, 2))
        else:
            late = jnp.where(
                q == 2, chunk_sum(kept_2, other_2, 0), chunk_sum(kept_1, other_1, 2)
            )
        return jnp.where(q < 2, early, late)

    far_up[...] = pair(2, 0).astype(BF16)
    far_down[...] = pair(2, 1).astype(BF16)
    free_up[...] = pair(1, 1).astype(BF16)
    free_down[...] = pair(3, 0).astype(BF16)
    held_up[...] = pair(1, 0)
    held_down[...] = pair(3, 1)
    for which in range(2):
        own[which] = pair(0, which)


def pass_on(place, held_up, held_down, got_up, got_down, next_up, next_down):
    next_up[...] = (held_up[...] + got_up[...].astype(F32)).astype(BF16)
    next_down[...] = (held_down[...] + got_down[...].astype(F32)).astype(BF16)


def activate(place, own, up_0, up_1, down_0, down_1, hidden_grad, hidden):
    half = hidden.shape[2]
    for which, up, down in ((0, up_0, down_0), (1, up_1, down_1)):
        total = own[which] + up[...].astype(F32) + down[...].astype(F32)
        activation, slope = gelu_parts(total[:, :half])
        hidden[which] = activation.astype(BF16)
        hidden_grad[which] = (total[:, half:] * slope).astype(BF16)


def assemble(place, own, up, down, far_up, far_down, out):
    y = place[0]
    far = lax.rem(y + 2, NY) * 2
    for which in range(2):
        out[y * 2 + which] = own[which]
        out[lax.rem(y + 3, NY) * 2 + which] = up[which]
        out[lax.rem(y + 1, NY) * 2 + which] = down[which]
    out[far] = far_up[0]
    out[far + 1] = far_down[0]


def backward_first(place, mine, weight, out):
    for k in range(NZ):
        out[k] = contract(mine[k], weight[...], (1, 1))


def backward_second(place, first, theirs, weight, far, out):
    for k in range(NZ):
        total = first[k] + contract(theirs[k], weight[...], (1, 1))
        if ORDER[k] == NZ // 2:
            far[0] = total[: far.shape[1]].astype(BF16)
            far[1] = total[far.shape[1] :].astype(BF16)
        else:
            out[k] = total


def weight_grad(scale, total, hidden_first, place, *refs):
    pieces, (mine, theirs, out, tokens_all) = refs[:total], refs[total:]
    width = tokens_all.shape[1]
    row = 0
    for piece in pieces:
        rows = piece.shape[0]
        tokens_all[pl.ds(row, rows)] = piece[:, width:] if hidden_first else piece[:, :width]
        row += rows
    core = place[1]
    half = mine.shape[2]
    for parts, at in ((mine, core * half), (theirs, (1 - core) * half)):
        joined = jnp.concatenate([parts[k] for k in range(NZ)], axis=0)
        side = pl.ds(pl.multiple_of(at, half), half)
        if hidden_first:
            out[side, :] = contract(joined, tokens_all[...], (0, 0)) * scale
        else:
            out[:, side] = contract(tokens_all[...], joined, (0, 0)) * scale


def after(value, *earlier):
    return lax.optimization_barrier((value, earlier))[0]


def per_device(normed, w_in, w_out, out_grad):
    rows, width = normed.shape
    chunk = rows * NX
    tokens = chunk * NZ
    units = w_in.shape[1]
    half_units = units // NC
    half = chunk // 2
    row = lax.axis_index("row")
    place = jnp.stack([row // NC, row % NC]).astype(jnp.int32)

    def project_group(group):
        pieces = [piece for d in group for piece in chunks[d]]
        counts = tuple(len(chunks[d]) for d in group)
        return on_core(
            functools.partial(project, counts),
            [((len(group), chunk, units), F32), ((len(group), chunk, units), BF16)],
            place, *pieces, *weights,
        )

    both = jnp.where(
        lax.broadcasted_iota(jnp.int32, (rows, 2 * width), 1) < width,
        jnp.pad(normed, ((0, 0), (0, width))),
        jnp.pad(out_grad, ((0, 0), (width, 0))),
    )
    line = [both] + [send_x(both, -e) for e in range(1, NX)]
    chunks = [[None, None] for _ in range(NZ)]
    for part in range(2):
        chunks[0][part] = jnp.concatenate(line[2 * part : 2 * part + 2], axis=0)
    weights = on_core(
        split_weights,
        [((width, half_units), BF16)] * 2 + [((half_units, width), BF16)] * 2,
        place, w_in, w_out,
    )
    for k in range(1, NZ // 2):
        for part in range(2):
            chunks[NZ - k][part] = send_z(chunks[(NZ + 1 - k) % NZ][part], 1)
            chunks[k][part] = send_z(chunks[k - 1][part], -1)
        if k == 1:
            chunks[NZ - 1][1], chunks[1][1], weights = lax.optimization_barrier(
                (chunks[NZ - 1][1], chunks[1][1], weights)
            )
    kept_0, away_0 = project_group(ROUNDS[0])
    kept_1, away_1 = project_group(ROUNDS[1])
    up, down = chunks[NZ // 2 + 1], chunks[NZ // 2 - 1]
    last = [send_z(up[0], 1), send_z(down[1], -1)]
    last, away_1 = lax.optimization_barrier((last, away_1))
    chunks[NZ // 2] = last
    other_0 = swap_core(away_0)
    other_1 = swap_core(away_1)
    kept_2, away_2 = project_group(ROUNDS[2])
    other_2 = swap_core(away_2)
    far_up, far_down, free_up, free_down, held_up, held_down, own = on_core(
        pair_sum,
        [((chunk, units), BF16)] * 4 + [((chunk, units), F32)] * 2 + [((2, chunk, units), F32)],
        place, kept_0, kept_1, kept_2, other_0, other_1, other_2,
    )
    got_up, got_down = send_y(far_up, 1), send_y(far_down, -1)
    free_up, free_down = send_y(free_up, 1), send_y(free_down, -1)
    next_up, next_down = on_core(
        pass_on, [((chunk, units), BF16)] * 2, place, held_up, held_down, got_up, got_down
    )
    grad_share, hidden_share = on_core(
        activate,
        [((2, chunk, half_units), BF16)] * 2,
        place, own, send_y(next_up, 1), free_up, free_down, send_y(next_down, -1),
    )

    def gathered(share, near, far):
        return on_core(assemble, [((NZ,) + share.shape[1:], BF16)], place, share, *near, *far)[0]

    near_grad = send_y(grad_share, 1), send_y(grad_share, -1)
    far_grad = send_y(near_grad[0][:1], 1), send_y(near_grad[1][1:], -1)
    grad_mine = gathered(grad_share, near_grad, far_grad)
    grad_theirs = swap_core(grad_mine)
    (first,) = on_core(
        backward_first, [((NZ, chunk, width), F32)], place, grad_mine, weights[0]
    )
    far, partial = on_core(
        backward_second,
        [((2, half, width), BF16), ((NZ, chunk, width), F32)],
        place, first, grad_theirs, weights[1],
    )

    pieces = [piece for d in ORDER for piece in chunks[d]]
    scale = float(tokens) ** (-0.5)

    def weight_call(hidden_first, shape, mine, theirs):
        operands = pieces + [mine, theirs]
        result = jax.ShapeDtypeStruct(shape, F32)
        return pl.pallas_call(
            functools.partial(weight_grad, scale, len(pieces), hidden_first),
            cost_estimate=cost(2 * tokens * shape[0] * shape[1], result, *operands),
            name="weight_grad",
            out_shape=result,
            in_specs=[pl.BlockSpec(memory_space=pltpu.SMEM)]
            + [pl.BlockSpec(memory_space=pltpu.VMEM)] * len(operands),
            out_specs=pl.BlockSpec(memory_space=pltpu.VMEM),
            scratch_shapes=[pltpu.VMEM((tokens, width), BF16)],
            compiler_params=pltpu.CompilerParams(vmem_limit_bytes=VMEM_BYTES),
        )(after(place, partial), *operands)

    part = lambda d: partial[ORDER.index(d)]
    up, down = send_z(far[0], 1), send_z(far[1], -1)
    up, down, hidden_share = lax.optimization_barrier((up, down, hidden_share))
    near_hidden = send_y(hidden_share, 1), send_y(hidden_share, -1)
    for k in range(NZ // 2 - 1, 0, -1):
        ahead, behind = part(k), part(NZ - k)
        if up.shape[0] == half:
            ahead = jnp.concatenate([ahead[:half] + up.astype(F32), ahead[half:]], axis=0)
            behind = jnp.concatenate([behind[:half], behind[half:] + down.astype(F32)], axis=0)
        else:
            ahead, behind = ahead + up.astype(F32), behind + down.astype(F32)
        ahead, behind = ahead.astype(BF16), behind.astype(BF16)
        if k == 1:
            ahead, behind, grad_mine = lax.optimization_barrier((ahead, behind, grad_mine))
            w_in_grad = weight_call(False, w_in.shape, grad_mine, grad_theirs)
        up, down = send_z(ahead, 1), send_z(behind, -1)
        if k == 1:
            up, down, w_in_grad = lax.optimization_barrier((up, down, w_in_grad))
        if k == 3:
            up, down, near_hidden = lax.optimization_barrier((up, down, near_hidden))
            far_hidden = send_y(near_hidden[0][:1], 1), send_y(near_hidden[1][1:], -1)
        if k == 2:
            hidden_mine = gathered(hidden_share, near_hidden, far_hidden)
            up, down, hidden_mine = lax.optimization_barrier((up, down, hidden_mine))
            hidden_theirs = swap_core(hidden_mine)
    w_out_grad = weight_call(True, w_out.shape, hidden_mine, hidden_theirs)
    up, down, hidden_theirs = lax.optimization_barrier((up, down, hidden_theirs))
    line = (part(0) + up.astype(F32) + down.astype(F32)).reshape(NX, rows, width)
    total = line[0]
    for e in range(1, NX):
        total = total + send_x(line[e].astype(BF16), e).astype(F32)
    return (total.astype(BF16), w_in_grad, w_out_grad)


def solution(mesh):
    in_specs = (P("col", "row"), P("row", "col"), P("col", "row"), P("col", "row"))
    out_specs = (P("col", "row"), P("row", "col"), P("col", "row"))
    return jax.shard_map(
        per_device, mesh=mesh, in_specs=in_specs, out_specs=out_specs, check_vma=False
    )
```

```python
import functools
import math

import jax
import jax.numpy as jnp
from jax import lax
from jax.experimental import pallas as pl
from jax.experimental.pallas import tpu as pltpu
from jax.sharding import PartitionSpec as P

NZ, NX, NY, NC = 8, 4, 4, 2
BF16, F32 = jnp.bfloat16, jnp.float32
VMEM_BYTES = 40 * 1024 * 1024

PLACES = ((1, 7), (2, 6), (0, 4), (3, 5))
ORDER = [d for pair in PLACES for d in pair]
ROUNDS = ((1, 7, 2, 6), (0, 3, 5), (4,))


def z_shift(step):
    return [(NX * z + x, NX * ((z + step) % NZ) + x) for z in range(NZ) for x in range(NX)]


def x_shift(step):
    return [(NX * z + x, NX * z + (x + step) % NX) for z in range(NZ) for x in range(NX)]


def y_shift(step):
    return [(NC * y + c, NC * ((y + step) % NY) + c) for y in range(NY) for c in range(NC)]


CORE_SWAP = [(r, r ^ 1) for r in range(NY * NC)]


def send_z(value, step):
    return lax.ppermute(value, "col", z_shift(step))


def send_x(value, step):
    return lax.ppermute(value, "col", x_shift(step))


def send_y(value, step):
    return lax.ppermute(value, "row", y_shift(step))


def swap_core(value):
    return lax.ppermute(value, "row", CORE_SWAP)


def cost(flops, *arrays):
    return pl.CostEstimate(
        flops=flops,
        transcendentals=0,
        bytes_accessed=sum(math.prod(a.shape) * a.dtype.itemsize for a in arrays),
    )


def on_core(kernel, outs, *operands, flops=0):
    shapes = [jax.ShapeDtypeStruct(shape, dtype) for shape, dtype in outs]
    return pl.pallas_call(
        kernel,
        cost_estimate=cost(flops, *operands, *shapes),
        name=getattr(kernel, "func", kernel).__name__,
        out_shape=shapes,
        in_specs=[pl.BlockSpec(memory_space=pltpu.SMEM)]
        + [pl.BlockSpec(memory_space=pltpu.VMEM)] * (len(operands) - 1),
        out_specs=[pl.BlockSpec(memory_space=pltpu.VMEM)] * len(outs),
        compiler_params=pltpu.CompilerParams(vmem_limit_bytes=VMEM_BYTES),
    )(*operands)


def contract(a, b, dims):
    return lax.dot_general(a, b, ((dims[:1], dims[1:]), ((), ())), preferred_element_type=F32)


def gelu_parts(preact):
    normal_cdf = 0.5 * (1.0 + lax.erf(preact * (1.0 / math.sqrt(2.0))))
    density = jnp.exp(-0.5 * preact * preact) * (1.0 / math.sqrt(2.0 * math.pi))
    return (preact * normal_cdf, normal_cdf + preact * density)


def split_weights(place, w_in, w_out, in_kept, in_away, out_kept, out_away):
    half = in_kept.shape[1]
    mine = place[1] == 0
    in_low, in_high = w_in[:, :half], w_in[:, half:]
    out_low, out_high = w_out[:half, :], w_out[half:, :]
    in_kept[...], in_away[...] = jnp.where(mine, in_low, in_high), jnp.where(mine, in_high, in_low)
    out_kept[...] = jnp.where(mine, out_low, out_high)
    out_away[...] = jnp.where(mine, out_high, out_low)


def project(counts, place, *refs):
    pieces, (in_kept, in_away, out_kept, out_away, kept, away) = (
        refs[: sum(counts)], refs[sum(counts) :]
    )
    width, half = in_kept.shape
    chunks, rows = kept.shape[:2]
    normed = jnp.concatenate([piece[:, :width] for piece in pieces], axis=0)
    grad = jnp.concatenate([piece[:, width:] for piece in pieces], axis=0)

    def store(out, side, value):
        for k in range(chunks):
            out[k, :, side] = value[k * rows : (k + 1) * rows].astype(out.dtype)

    left, right = pl.ds(0, half), pl.ds(half, half)
    store(away, left, contract(normed, in_away[...], (1, 0)))
    store(away, right, contract(grad, out_away[...], (1, 1)))
    store(kept, left, contract(normed, in_kept[...], (1, 0)))
    store(kept, right, contract(grad, out_kept[...], (1, 1)))


def pair_sum(
    place, kept_0, kept_1, kept_2, other_0, other_1, other_2,
    far_up, far_down, free_up, free_down, held_up, held_down, own,
):
    y = place[0]

    def chunk_sum(kept, other, at):
        return kept[at] + other[at].astype(F32)

    def pair(step, which):
        q = lax.rem(y + step, NY)
        early = chunk_sum(kept_0, other_0, lax.rem(q, 2) * 2 + which)
        if which == 0:
            late = chunk_sum(kept_1, other_1, lax.rem(q, 2))
        else:
            late = jnp.where(
                q == 2, chunk_sum(kept_2, other_2, 0), chunk_sum(kept_1, other_1, 2)
            )
        return jnp.where(q < 2, early, late)

    far_up[...] = pair(2, 0).astype(BF16)
    far_down[...] = pair(2, 1).astype(BF16)
    free_up[...] = pair(1, 1).astype(BF16)
    free_down[...] = pair(3, 0).astype(BF16)
    held_up[...] = pair(1, 0)
    held_down[...] = pair(3, 1)
    for which in range(2):
        own[which] = pair(0, which)


def pass_on(place, held_up, held_down, got_up, got_down, next_up, next_down):
    next_up[...] = (held_up[...] + got_up[...].astype(F32)).astype(BF16)
    next_down[...] = (held_down[...] + got_down[...].astype(F32)).astype(BF16)


def activate(place, own, up_0, up_1, down_0, down_1, hidden_grad, hidden):
    half = hidden.shape[2]
    for which, up, down in ((0, up_0, down_0), (1, up_1, down_1)):
        total = own[which] + up[...].astype(F32) + down[...].astype(F32)
        activation, slope = gelu_parts(total[:, :half])
        hidden[which] = activation.astype(BF16)
        hidden_grad[which] = (total[:, half:] * slope).astype(BF16)


def assemble(place, own, up, down, far_up, far_down, out):
    y = place[0]
    far = lax.rem(y + 2, NY) * 2
    for which in range(2):
        out[y * 2 + which] = own[which]
        out[lax.rem(y + 3, NY) * 2 + which] = up[which]
        out[lax.rem(y + 1, NY) * 2 + which] = down[which]
    out[far] = far_up[0]
    out[far + 1] = far_down[0]


def backward_first(place, mine, weight, out):
    for k in range(NZ):
        out[k] = contract(mine[k], weight[...], (1, 1))


def backward_second(place, first, theirs, weight, far, out):
    for k in range(NZ):
        total = first[k] + contract(theirs[k], weight[...], (1, 1))
        if ORDER[k] == NZ // 2:
            far[0] = total[: far.shape[1]].astype(BF16)
            far[1] = total[far.shape[1] :].astype(BF16)
        else:
            out[k] = total


def weight_grad(scale, total, hidden_first, place, *refs):
    pieces, (mine, theirs, out, tokens_all) = refs[:total], refs[total:]
    width = tokens_all.shape[1]
    row = 0
    for piece in pieces:
        rows = piece.shape[0]
        tokens_all[pl.ds(row, rows)] = piece[:, width:] if hidden_first else piece[:, :width]
        row += rows
    core = place[1]
    half = mine.shape[2]
    for parts, at in ((mine, core * half), (theirs, (1 - core) * half)):
        joined = jnp.concatenate([parts[k] for k in range(NZ)], axis=0)
        side = pl.ds(pl.multiple_of(at, half), half)
        if hidden_first:
            out[side, :] = contract(joined, tokens_all[...], (0, 0)) * scale
        else:
            out[:, side] = contract(tokens_all[...], joined, (0, 0)) * scale


def after(value, *earlier):
    return lax.optimization_barrier((value, earlier))[0]


def per_device(normed, w_in, w_out, out_grad):
    rows, width = normed.shape
    chunk = rows * NX
    tokens = chunk * NZ
    units = w_in.shape[1]
    half_units = units // NC
    half = chunk // 2
    row = lax.axis_index("row")
    place = jnp.stack([row // NC, row % NC]).astype(jnp.int32)

    def project_group(group):
        pieces = [piece for d in group for piece in chunks[d]]
        counts = tuple(len(chunks[d]) for d in group)
        return on_core(
            functools.partial(project, counts),
            [((len(group), chunk, units), F32), ((len(group), chunk, units), BF16)],
            place, *pieces, *weights,
        )

    both = jnp.where(
        lax.broadcasted_iota(jnp.int32, (rows, 2 * width), 1) < width,
        jnp.pad(normed, ((0, 0), (0, width))),
        jnp.pad(out_grad, ((0, 0), (width, 0))),
    )
    line = [both] + [send_x(both, -e) for e in range(1, NX)]
    weights = on_core(
        split_weights,
        [((width, half_units), BF16)] * 2 + [((half_units, width), BF16)] * 2,
        place, w_in, w_out,
    )
    line, weights = lax.optimization_barrier((line, weights))
    chunks = [[None, None] for _ in range(NZ)]
    for part in range(2):
        chunks[0][part] = jnp.concatenate(line[2 * part : 2 * part + 2], axis=0)
    for k in range(1, NZ // 2):
        for part in range(2):
            chunks[NZ - k][part] = send_z(chunks[(NZ + 1 - k) % NZ][part], 1)
            chunks[k][part] = send_z(chunks[k - 1][part], -1)
    kept_0, away_0 = project_group(ROUNDS[0])
    kept_1, away_1 = project_group(ROUNDS[1])
    up, down = chunks[NZ // 2 + 1], chunks[NZ // 2 - 1]
    last = [send_z(up[0], 1), send_z(down[1], -1)]
    last, away_1 = lax.optimization_barrier((last, away_1))
    chunks[NZ // 2] = last
    other_0 = swap_core(away_0)
    other_1 = swap_core(away_1)
    kept_2, away_2 = project_group(ROUNDS[2])
    other_2 = swap_core(away_2)
    far_up, far_down, free_up, free_down, held_up, held_down, own = on_core(
        pair_sum,
        [((chunk, units), BF16)] * 4 + [((chunk, units), F32)] * 2 + [((2, chunk, units), F32)],
        place, kept_0, kept_1, kept_2, other_0, other_1, other_2,
    )
    got_up, got_down = send_y(far_up, 1), send_y(far_down, -1)
    free_up, free_down = send_y(free_up, 1), send_y(free_down, -1)
    next_up, next_down = on_core(
        pass_on, [((chunk, units), BF16)] * 2, place, held_up, held_down, got_up, got_down
    )
    grad_share, hidden_share = on_core(
        activate,
        [((2, chunk, half_units), BF16)] * 2,
        place, own, send_y(next_up, 1), free_up, free_down, send_y(next_down, -1),
    )

    def gathered(share, near, far):
        return on_core(assemble, [((NZ,) + share.shape[1:], BF16)], place, share, *near, *far)[0]

    near_grad = send_y(grad_share, 1), send_y(grad_share, -1)
    far_grad = send_y(near_grad[0][:1], 1), send_y(near_grad[1][1:], -1)
    grad_mine = gathered(grad_share, near_grad, far_grad)
    grad_theirs = swap_core(grad_mine)
    (first,) = on_core(
        backward_first, [((NZ, chunk, width), F32)], place, grad_mine, weights[0]
    )
    far, partial = on_core(
        backward_second,
        [((2, half, width), BF16), ((NZ, chunk, width), F32)],
        place, first, grad_theirs, weights[1],
    )

    pieces = [piece for d in ORDER for piece in chunks[d]]
    scale = float(tokens) ** (-0.5)

    def weight_call(hidden_first, shape, mine, theirs):
        operands = pieces + [mine, theirs]
        result = jax.ShapeDtypeStruct(shape, F32)
        return pl.pallas_call(
            functools.partial(weight_grad, scale, len(pieces), hidden_first),
            cost_estimate=cost(2 * tokens * shape[0] * shape[1], result, *operands),
            name="weight_grad",
            out_shape=result,
            in_specs=[pl.BlockSpec(memory_space=pltpu.SMEM)]
            + [pl.BlockSpec(memory_space=pltpu.VMEM)] * len(operands),
            out_specs=pl.BlockSpec(memory_space=pltpu.VMEM),
            scratch_shapes=[pltpu.VMEM((tokens, width), BF16)],
            compiler_params=pltpu.CompilerParams(vmem_limit_bytes=VMEM_BYTES),
        )(after(place, partial), *operands)

    part = lambda d: partial[ORDER.index(d)]
    up, down = send_z(far[0], 1), send_z(far[1], -1)
    up, down, hidden_share = lax.optimization_barrier((up, down, hidden_share))
    near_hidden = send_y(hidden_share, 1), send_y(hidden_share, -1)
    for k in range(NZ // 2 - 1, 0, -1):
        ahead, behind = part(k), part(NZ - k)
        if up.shape[0] == half:
            ahead = jnp.concatenate([ahead[:half] + up.astype(F32), ahead[half:]], axis=0)
            behind = jnp.concatenate([behind[:half], behind[half:] + down.astype(F32)], axis=0)
        else:
            ahead, behind = ahead + up.astype(F32), behind + down.astype(F32)
        ahead, behind = ahead.astype(BF16), behind.astype(BF16)
        if k == 1:
            ahead, behind, grad_mine = lax.optimization_barrier((ahead, behind, grad_mine))
            w_in_grad = weight_call(False, w_in.shape, grad_mine, grad_theirs)
        up, down = send_z(ahead, 1), send_z(behind, -1)
        if k == 1:
            up, down, w_in_grad = lax.optimization_barrier((up, down, w_in_grad))
        if k == 3:
            up, down, near_hidden = lax.optimization_barrier((up, down, near_hidden))
            far_hidden = send_y(near_hidden[0][:1], 1), send_y(near_hidden[1][1:], -1)
        if k == 2:
            hidden_mine = gathered(hidden_share, near_hidden, far_hidden)
            up, down, hidden_mine = lax.optimization_barrier((up, down, hidden_mine))
            hidden_theirs = swap_core(hidden_mine)
    w_out_grad = weight_call(True, w_out.shape, hidden_mine, hidden_theirs)
    up, down, hidden_theirs = lax.optimization_barrier((up, down, hidden_theirs))
    line = (part(0) + up.astype(F32) + down.astype(F32)).reshape(NX, rows, width)
    total = line[0]
    for e in range(1, NX):
        total = total + send_x(line[e].astype(BF16), e).astype(F32)
    return (total.astype(BF16), w_in_grad, w_out_grad)


def solution(mesh):
    in_specs = (P("col", "row"), P("row", "col"), P("col", "row"), P("col", "row"))
    out_specs = (P("col", "row"), P("row", "col"), P("col", "row"))
    return jax.shard_map(
        per_device, mesh=mesh, in_specs=in_specs, out_specs=out_specs, check_vma=False
    )
```

```python
import functools
import math

import jax
import jax.numpy as jnp
from jax import lax
from jax.experimental import pallas as pl
from jax.experimental.pallas import tpu as pltpu
from jax.sharding import PartitionSpec as P

NZ, NX, NY, NC = 8, 4, 4, 2
BF16, F32 = jnp.bfloat16, jnp.float32
VMEM_BYTES = 40 * 1024 * 1024

PLACES = ((1, 7), (2, 6), (0, 4), (3, 5))
ORDER = [d for pair in PLACES for d in pair]
ROUNDS = ((1, 7, 2, 6), (0, 3, 5), (4,))


def z_shift(step):
    return [(NX * z + x, NX * ((z + step) % NZ) + x) for z in range(NZ) for x in range(NX)]


def x_shift(step):
    return [(NX * z + x, NX * z + (x + step) % NX) for z in range(NZ) for x in range(NX)]


def y_shift(step):
    return [(NC * y + c, NC * ((y + step) % NY) + c) for y in range(NY) for c in range(NC)]


CORE_SWAP = [(r, r ^ 1) for r in range(NY * NC)]


def send_z(value, step):
    return lax.ppermute(value, "col", z_shift(step))


def send_x(value, step):
    return lax.ppermute(value, "col", x_shift(step))


def send_y(value, step):
    return lax.ppermute(value, "row", y_shift(step))


def swap_core(value):
    return lax.ppermute(value, "row", CORE_SWAP)


def cost(flops, *arrays):
    return pl.CostEstimate(
        flops=flops,
        transcendentals=0,
        bytes_accessed=sum(math.prod(a.shape) * a.dtype.itemsize for a in arrays),
    )


def on_core(kernel, outs, *operands, flops=0):
    shapes = [jax.ShapeDtypeStruct(shape, dtype) for shape, dtype in outs]
    return pl.pallas_call(
        kernel,
        cost_estimate=cost(flops, *operands, *shapes),
        name=getattr(kernel, "func", kernel).__name__,
        out_shape=shapes,
        in_specs=[pl.BlockSpec(memory_space=pltpu.SMEM)]
        + [pl.BlockSpec(memory_space=pltpu.VMEM)] * (len(operands) - 1),
        out_specs=[pl.BlockSpec(memory_space=pltpu.VMEM)] * len(outs),
        compiler_params=pltpu.CompilerParams(vmem_limit_bytes=VMEM_BYTES),
    )(*operands)


def contract(a, b, dims):
    return lax.dot_general(a, b, ((dims[:1], dims[1:]), ((), ())), preferred_element_type=F32)


def gelu_parts(preact):
    normal_cdf = 0.5 * (1.0 + lax.erf(preact * (1.0 / math.sqrt(2.0))))
    density = jnp.exp(-0.5 * preact * preact) * (1.0 / math.sqrt(2.0 * math.pi))
    return (preact * normal_cdf, normal_cdf + preact * density)


def split_weights(place, w_in, w_out, in_kept, in_away, out_kept, out_away):
    half = in_kept.shape[1]
    mine = place[1] == 0
    in_low, in_high = w_in[:, :half], w_in[:, half:]
    out_low, out_high = w_out[:half, :], w_out[half:, :]
    in_kept[...], in_away[...] = jnp.where(mine, in_low, in_high), jnp.where(mine, in_high, in_low)
    out_kept[...] = jnp.where(mine, out_low, out_high)
    out_away[...] = jnp.where(mine, out_high, out_low)


def project(counts, place, *refs):
    pieces, (in_kept, in_away, out_kept, out_away, kept, away) = (
        refs[: sum(counts)], refs[sum(counts) :]
    )
    width, half = in_kept.shape
    chunks, rows = kept.shape[:2]
    normed = jnp.concatenate([piece[:, :width] for piece in pieces], axis=0)
    grad = jnp.concatenate([piece[:, width:] for piece in pieces], axis=0)

    def store(out, side, value):
        for k in range(chunks):
            out[k, :, side] = value[k * rows : (k + 1) * rows].astype(out.dtype)

    left, right = pl.ds(0, half), pl.ds(half, half)
    store(away, left, contract(normed, in_away[...], (1, 0)))
    store(away, right, contract(grad, out_away[...], (1, 1)))
    store(kept, left, contract(normed, in_kept[...], (1, 0)))
    store(kept, right, contract(grad, out_kept[...], (1, 1)))


def pair_sum(
    place, kept_0, kept_1, kept_2, other_0, other_1, other_2,
    far_up, far_down, free_up, free_down, held_up, held_down, own,
):
    y = place[0]

    def chunk_sum(kept, other, at):
        return kept[at] + other[at].astype(F32)

    def pair(step, which):
        q = lax.rem(y + step, NY)
        early = chunk_sum(kept_0, other_0, lax.rem(q, 2) * 2 + which)
        if which == 0:
            late = chunk_sum(kept_1, other_1, lax.rem(q, 2))
        else:
            late = jnp.where(
                q == 2, chunk_sum(kept_2, other_2, 0), chunk_sum(kept_1, other_1, 2)
            )
        return jnp.where(q < 2, early, late)

    far_up[...] = pair(2, 0).astype(BF16)
    far_down[...] = pair(2, 1).astype(BF16)
    free_up[...] = pair(1, 1).astype(BF16)
    free_down[...] = pair(3, 0).astype(BF16)
    held_up[...] = pair(1, 0)
    held_down[...] = pair(3, 1)
    for which in range(2):
        own[which] = pair(0, which)


def pass_on(place, held_up, held_down, got_up, got_down, next_up, next_down):
    next_up[...] = (held_up[...] + got_up[...].astype(F32)).astype(BF16)
    next_down[...] = (held_down[...] + got_down[...].astype(F32)).astype(BF16)


def activate(place, own, up_0, up_1, down_0, down_1, grad_0, grad_1, hidden):
    half = hidden.shape[2]
    for which, up, down, grad in ((0, up_0, down_0, grad_0), (1, up_1, down_1, grad_1)):
        total = own[which] + up[...].astype(F32) + down[...].astype(F32)
        activation, slope = gelu_parts(total[:, :half])
        hidden[which] = activation.astype(BF16)
        grad[...] = (total[:, half:] * slope).astype(BF16)


def assemble_halves(place, *refs):
    pieces, out = refs[:-1], refs[-1]
    for pair, step in enumerate((0, 3, 1, 2)):
        at = lax.rem(place[0] + step, NY) * 2
        out[at] = pieces[2 * pair][...]
        out[at + 1] = pieces[2 * pair + 1][...]


def assemble(place, own, up, down, far_up, far_down, out):
    y = place[0]
    far = lax.rem(y + 2, NY) * 2
    for which in range(2):
        out[y * 2 + which] = own[which]
        out[lax.rem(y + 3, NY) * 2 + which] = up[which]
        out[lax.rem(y + 1, NY) * 2 + which] = down[which]
    out[far] = far_up[0]
    out[far + 1] = far_down[0]


def backward_first(place, mine, weight, out):
    for k in range(NZ):
        out[k] = contract(mine[k], weight[...], (1, 1))


def backward_second(place, first, theirs, weight, far, out):
    for k in range(NZ):
        total = first[k] + contract(theirs[k], weight[...], (1, 1))
        if ORDER[k] == NZ // 2:
            far[0] = total[: far.shape[1]].astype(BF16)
            far[1] = total[far.shape[1] :].astype(BF16)
        else:
            out[k] = total


def weight_grad(scale, total, hidden_first, place, *refs):
    pieces, (mine, theirs, out, tokens_all) = refs[:total], refs[total:]
    width = tokens_all.shape[1]
    row = 0
    for piece in pieces:
        rows = piece.shape[0]
        tokens_all[pl.ds(row, rows)] = piece[:, width:] if hidden_first else piece[:, :width]
        row += rows
    core = place[1]
    half = mine.shape[2]
    for parts, at in ((mine, core * half), (theirs, (1 - core) * half)):
        joined = jnp.concatenate([parts[k] for k in range(NZ)], axis=0)
        side = pl.ds(pl.multiple_of(at, half), half)
        if hidden_first:
            out[side, :] = contract(joined, tokens_all[...], (0, 0)) * scale
        else:
            out[:, side] = contract(tokens_all[...], joined, (0, 0)) * scale


def after(value, *earlier):
    return lax.optimization_barrier((value, earlier))[0]


def per_device(normed, w_in, w_out, out_grad):
    rows, width = normed.shape
    chunk = rows * NX
    tokens = chunk * NZ
    units = w_in.shape[1]
    half_units = units // NC
    half = chunk // 2
    row = lax.axis_index("row")
    place = jnp.stack([row // NC, row % NC]).astype(jnp.int32)

    def project_group(group):
        pieces = [piece for d in group for piece in chunks[d]]
        counts = tuple(len(chunks[d]) for d in group)
        return on_core(
            functools.partial(project, counts),
            [((len(group), chunk, units), F32), ((len(group), chunk, units), BF16)],
            place, *pieces, *weights,
        )

    both = jnp.where(
        lax.broadcasted_iota(jnp.int32, (rows, 2 * width), 1) < width,
        jnp.pad(normed, ((0, 0), (0, width))),
        jnp.pad(out_grad, ((0, 0), (width, 0))),
    )
    line = [both] + [send_x(both, -e) for e in range(1, NX)]
    weights = on_core(
        split_weights,
        [((width, half_units), BF16)] * 2 + [((half_units, width), BF16)] * 2,
        place, w_in, w_out,
    )
    line, weights = lax.optimization_barrier((line, weights))
    chunks = [[None, None] for _ in range(NZ)]
    for part in range(2):
        chunks[0][part] = jnp.concatenate(line[2 * part : 2 * part + 2], axis=0)
    for k in range(1, NZ // 2):
        for part in range(2):
            chunks[NZ - k][part] = send_z(chunks[(NZ + 1 - k) % NZ][part], 1)
            chunks[k][part] = send_z(chunks[k - 1][part], -1)
    kept_0, away_0 = project_group(ROUNDS[0])
    kept_1, away_1 = project_group(ROUNDS[1])
    up, down = chunks[NZ // 2 + 1], chunks[NZ // 2 - 1]
    last = [send_z(up[0], 1), send_z(down[1], -1)]
    last, away_1 = lax.optimization_barrier((last, away_1))
    chunks[NZ // 2] = last
    other_0 = swap_core(away_0)
    other_1 = swap_core(away_1)
    kept_2, away_2 = project_group(ROUNDS[2])
    other_2 = swap_core(away_2)
    far_up, far_down, free_up, free_down, held_up, held_down, own = on_core(
        pair_sum,
        [((chunk, units), BF16)] * 4 + [((chunk, units), F32)] * 2 + [((2, chunk, units), F32)],
        place, kept_0, kept_1, kept_2, other_0, other_1, other_2,
    )
    got_up, got_down = send_y(far_up, 1), send_y(far_down, -1)
    free_up, free_down = send_y(free_up, 1), send_y(free_down, -1)
    next_up, next_down = on_core(
        pass_on, [((chunk, units), BF16)] * 2, place, held_up, held_down, got_up, got_down
    )
    grad_0, grad_1, hidden_share = on_core(
        activate,
        [((chunk, half_units), BF16)] * 2 + [((2, chunk, half_units), BF16)],
        place, own, send_y(next_up, 1), free_up, free_down, send_y(next_down, -1),
    )

    def gathered(share, near, far):
        return on_core(assemble, [((NZ,) + share.shape[1:], BF16)], place, share, *near, *far)[0]

    from_behind, from_ahead = [send_y(grad_0, 1)], [send_y(grad_1, -1)]
    far_grad = [send_y(from_behind[0], 1), send_y(from_ahead[0], -1)]
    from_behind.append(send_y(grad_1, 1))
    from_ahead.insert(0, send_y(grad_0, -1))
    (grad_mine,) = on_core(
        assemble_halves,
        [((NZ, chunk, half_units), BF16)],
        place, grad_0, grad_1, *from_behind, *from_ahead, *far_grad,
    )
    grad_theirs = swap_core(grad_mine)
    (first,) = on_core(
        backward_first, [((NZ, chunk, width), F32)], place, grad_mine, weights[0]
    )
    far, partial = on_core(
        backward_second,
        [((2, half, width), BF16), ((NZ, chunk, width), F32)],
        place, first, grad_theirs, weights[1],
    )

    pieces = [piece for d in ORDER for piece in chunks[d]]
    scale = float(tokens) ** (-0.5)

    def weight_call(hidden_first, shape, mine, theirs):
        operands = pieces + [mine, theirs]
        result = jax.ShapeDtypeStruct(shape, F32)
        return pl.pallas_call(
            functools.partial(weight_grad, scale, len(pieces), hidden_first),
            cost_estimate=cost(2 * tokens * shape[0] * shape[1], result, *operands),
            name="weight_grad",
            out_shape=result,
            in_specs=[pl.BlockSpec(memory_space=pltpu.SMEM)]
            + [pl.BlockSpec(memory_space=pltpu.VMEM)] * len(operands),
            out_specs=pl.BlockSpec(memory_space=pltpu.VMEM),
            scratch_shapes=[pltpu.VMEM((tokens, width), BF16)],
            compiler_params=pltpu.CompilerParams(vmem_limit_bytes=VMEM_BYTES),
        )(after(place, partial), *operands)

    part = lambda d: partial[ORDER.index(d)]
    up, down = send_z(far[0], 1), send_z(far[1], -1)
    up, down, hidden_share = lax.optimization_barrier((up, down, hidden_share))
    near_hidden = send_y(hidden_share, 1), send_y(hidden_share, -1)
    for k in range(NZ // 2 - 1, 0, -1):
        ahead, behind = part(k), part(NZ - k)
        if up.shape[0] == half:
            ahead = jnp.concatenate([ahead[:half] + up.astype(F32), ahead[half:]], axis=0)
            behind = jnp.concatenate([behind[:half], behind[half:] + down.astype(F32)], axis=0)
        else:
            ahead, behind = ahead + up.astype(F32), behind + down.astype(F32)
        ahead, behind = ahead.astype(BF16), behind.astype(BF16)
        if k == 1:
            ahead, behind, grad_mine = lax.optimization_barrier((ahead, behind, grad_mine))
            w_in_grad = weight_call(False, w_in.shape, grad_mine, grad_theirs)
        up, down = send_z(ahead, 1), send_z(behind, -1)
        if k == 1:
            up, down, w_in_grad = lax.optimization_barrier((up, down, w_in_grad))
        if k == 3:
            up, down, near_hidden = lax.optimization_barrier((up, down, near_hidden))
            far_hidden = send_y(near_hidden[0][:1], 1), send_y(near_hidden[1][1:], -1)
        if k == 2:
            hidden_mine = gathered(hidden_share, near_hidden, far_hidden)
            up, down, hidden_mine = lax.optimization_barrier((up, down, hidden_mine))
            hidden_theirs = swap_core(hidden_mine)
    w_out_grad = weight_call(True, w_out.shape, hidden_mine, hidden_theirs)
    up, down, hidden_theirs = lax.optimization_barrier((up, down, hidden_theirs))
    line = (part(0) + up.astype(F32) + down.astype(F32)).reshape(NX, rows, width)
    total = line[0]
    for e in range(1, NX):
        total = total + send_x(line[e].astype(BF16), e).astype(F32)
    return (total.astype(BF16), w_in_grad, w_out_grad)


def solution(mesh):
    in_specs = (P("col", "row"), P("row", "col"), P("col", "row"), P("col", "row"))
    out_specs = (P("col", "row"), P("row", "col"), P("col", "row"))
    return jax.shard_map(
        per_device, mesh=mesh, in_specs=in_specs, out_specs=out_specs, check_vma=False
    )
```
